512 devices in a mesh: pipe: 16 (over z_lo, x), ctx: 16 (over y, z_hi), head: 2 (over core).
Axes of the slice: x: 4, y: 8, z: 8 (z_hi: 2, z_lo: 4; z = z_hi * 4 + z_lo), core: 2. Of those that a mesh axis runs over, the one named last changes fastest.
Arguments:
- queries: bfloat16 [16, 2048, 64, 128], P('pipe', 'ctx', 'head'), may hold values from -160 to 160
- key_heads: bfloat16 [16, 2048, 8, 128], P('pipe', 'ctx', 'head'), may hold values from -6 to 6
- value_heads: bfloat16 [16, 2048, 8, 128], P('pipe', 'ctx', 'head'), may hold values from -6 to 6
- forward_out: bfloat16 [16, 2048, 64, 128], P('pipe', 'ctx', 'head'), may hold values from -4 to 4
- output_grad: bfloat16 [16, 2048, 64, 128], P('pipe', 'ctx', 'head'), may hold values from -6 to 6
- block_order: int32 [32], replicated, may hold values from 0 to 31, each once
Outputs:
- key_grad: bfloat16 [16, 2048, 8, 128], P('pipe', 'ctx', 'head')
- value_grad: bfloat16 [16, 2048, 8, 128], P('pipe', 'ctx', 'head')
- handed: bfloat16 [16, 2048, 64, 128], P('pipe', 'ctx', 'head')
The draws below stay inside these ranges and needn't reach their ends.
Inputs may be any that keep to these rules, and one draw needn't show every extreme that they name: `block_order`: every half-block number appears exactly once.
All inputs are finite; a program needn't handle non-finite values.
Results may differ from the reference program's by a relative error of at most 0.012.
The reference program's roundings to bfloat16 on the way count: a program that leaves them out, or rounds other values in their place, can miss the bound.
Values may be sent and summed in bfloat16 or wider, within the bound.
A program may use at most 64 MiB of HBM per device.

```python
import math
import jax
import jax.numpy as jnp
from jax import lax

QH = 64
KVH = 8
HD = 128
HALF = 64
SEQ = 2048
N_PIPE = 16
N_CTX = 16


def draw_common(key):
    base = jax.random.fold_in(key, 11)
    key_draw, query_draw = jax.random.split(base, 2)
    key_vals = jnp.clip(jax.random.normal(key_draw, (N_PIPE, SEQ, KVH, HD), jnp.float32), -6.0, 6.0)
    query_vals = jnp.clip(jax.random.normal(query_draw, (N_PIPE, SEQ, QH, HD), jnp.float32), -6.0, 6.0)
    return (key_vals, query_vals)


def draw_queries(key, part):
    key_vals, query_vals = draw_common(key)
    return query_vals.astype(jnp.bfloat16)


def draw_key_heads(key, part):
    key_vals, query_vals = draw_common(key)
    return key_vals.astype(jnp.bfloat16)


def block_scale(key, extent, cuts, low, top_value):
    def one(axis_at, shards_of):
        steps = jax.random.uniform(jax.random.fold_in(jax.random.fold_in(key, 6), axis_at), (shards_of,), jnp.float32, low / len(cuts), top_value / len(cuts))
        return jnp.repeat(jnp.exp(steps), extent[axis_at] // shards_of).reshape((-1,) + (1,) * (len(extent) - axis_at - 1))

    level = one(*cuts[0])
    for cut in cuts[1:]:
        level = level * one(*cut)
    return level


def gaussian(key, extent, scale, limit, shards=(), kind=jnp.bfloat16):
    values = scale * jax.random.normal(key, extent, jnp.float32)
    if shards:
        values = values * block_scale(key, extent, shards, -0.22, 0.18)
    return jnp.clip(values, -limit, limit).astype(kind)


def setup_inputs(seed: int = 0) -> dict:
    keys = jax.random.split(jax.random.key(seed), 7)
    queries = draw_queries(jax.random.fold_in(keys[6], 71), 0)
    key_heads = draw_key_heads(jax.random.fold_in(keys[6], 71), 0)
    value_heads = gaussian(keys[2], (N_PIPE, SEQ, KVH, HD), 1.0, 6.0, ((0, 16), (1, 16), (2, 2)))
    forward_out = gaussian(keys[3], (N_PIPE, SEQ, QH, HD), 0.5, 4.0, ((0, 16), (1, 16), (2, 2)))
    output_grad = gaussian(keys[4], (N_PIPE, SEQ, QH, HD), 1.0, 6.0, ((0, 16), (1, 16), (2, 2)))
    block_order = jax.random.permutation(keys[5], 2 * N_CTX).astype(jnp.int32)
    return {"queries": queries, "key_heads": key_heads, "value_heads": value_heads, "forward_out": forward_out, "output_grad": output_grad, "block_order": block_order}


NEG = -1e+30

def hadamard(size_in):
    indices = jnp.arange(size_in, dtype=jnp.int32)
    parity = jnp.zeros((size_in, size_in), jnp.int32)
    for bit_place in range(size_in.bit_length() - 1):
        digit = indices // 2 ** bit_place % 2
        parity = parity + digit[:, None] * digit[None, :]
    parity = parity % 2
    return (1.0 - 2.0 * parity.astype(jnp.float32)) / math.sqrt(size_in)

def rotate(values, rotation):
    return jnp.dot(values.astype(jnp.float32), rotation, precision=lax.Precision.HIGHEST).astype(jnp.bfloat16)

def reference(queries, key_heads, value_heads, forward_out, output_grad, block_order):
    rotation = hadamard(HD)
    score_scale = 1.0 / math.sqrt(HD)
    per_group = QH // KVH
    seq_rows = jnp.arange(SEQ, dtype=jnp.int32)
    positions = jnp.repeat(block_order.astype(jnp.int32), HALF) * HALF + seq_rows % HALF
    visible = positions[None, :] <= positions[:, None]

    def stack_query(array):
        return array.reshape(N_PIPE, SEQ, KVH, per_group, HD).transpose(0, 2, 1, 3, 4).reshape(N_PIPE * KVH, SEQ, per_group, HD)

    def stack_key(array):
        return array.transpose(0, 2, 1, 3).reshape(N_PIPE * KVH, SEQ, HD)

    def one_group(items):
        q_in, k_in, v_in, o_in, g_in = items
        q_rot = rotate(q_in, rotation)
        k_rot = rotate(k_in, rotation)
        scores = jnp.einsum('igd,jd->gij', q_rot.astype(jnp.float32), k_rot.astype(jnp.float32)) * score_scale
        scores = jnp.where(visible[None], scores, NEG)
        row_top = lax.optimization_barrier(jnp.max(scores, -1, keepdims=True))
        row_lse = row_top + jnp.log(lax.optimization_barrier(jnp.sum(jnp.exp(scores - row_top), -1, keepdims=True)))
        weights = jnp.exp(scores - row_lse)
        grad_f = g_in.astype(jnp.float32)
        row_delta = lax.optimization_barrier(jnp.sum(grad_f * o_in.astype(jnp.float32), -1)).T
        weight_grad = jnp.einsum('igd,jd->gij', grad_f, v_in.astype(jnp.float32))
        dscore = (weights * (weight_grad - row_delta[..., None])).astype(jnp.bfloat16)
        weights_low = weights.astype(jnp.bfloat16)
        dq_rot = jnp.einsum('gij,jd->igd', dscore.astype(jnp.float32), k_rot.astype(jnp.float32)) * score_scale
        dk_rot = jnp.einsum('gij,igd->jd', dscore.astype(jnp.float32), q_rot.astype(jnp.float32)) * score_scale
        dv_sum = jnp.einsum('gij,igd->jd', weights_low.astype(jnp.float32), grad_f)
        dq_full = jnp.dot(dq_rot.reshape(-1, HD), rotation.T, precision=lax.Precision.HIGHEST).reshape(SEQ, per_group, HD)
        dk_full = jnp.dot(dk_rot, rotation.T, precision=lax.Precision.HIGHEST)
        handed_here = (grad_f + dq_full).astype(jnp.bfloat16)
        return (dk_full.astype(jnp.bfloat16), dv_sum.astype(jnp.bfloat16), handed_here)
    dk_all, dv_all, handed_all = lax.map(one_group, (stack_query(queries), stack_key(key_heads), stack_key(value_heads), stack_query(forward_out), stack_query(output_grad)))
    key_grad = dk_all.reshape(N_PIPE, KVH, SEQ, HD).transpose(0, 2, 1, 3)
    value_grad = dv_all.reshape(N_PIPE, KVH, SEQ, HD).transpose(0, 2, 1, 3)
    handed_all = handed_all.reshape(N_PIPE, KVH, SEQ, per_group, HD).transpose(0, 2, 1, 3, 4).reshape(N_PIPE, SEQ, QH, HD)
    handed = jnp.concatenate([handed_all[1:], jnp.zeros_like(handed_all[:1])], axis=0)
    return (key_grad, value_grad, handed)
```

```python
import math

import jax
import jax.numpy as jnp
import numpy as np
from jax import lax
from jax.experimental import pallas as pl
from jax.experimental.pallas import tpu as pltpu
from jax.sharding import PartitionSpec as P

MESH = pl.DeviceIdType.MESH
NEG = -1e30
F32 = jnp.float32
BF16 = jnp.bfloat16
NY = 8
LOOK = 2
CHUNK = 256


def signs(size):
    index = np.arange(size)
    ands = index[:, None] & index[None, :]
    parity = np.zeros((size, size), np.int64)
    for bit in range(size.bit_length() - 1):
        parity ^= (ands >> bit) & 1
    return 1.0 - 2.0 * parity


def dot(a, b):
    return jnp.dot(a, b, preferred_element_type=F32)


def split3(x):
    a = x.astype(BF16)
    r = x - a.astype(F32)
    b = r.astype(BF16)
    c = (r - b.astype(F32)).astype(BF16)
    return a, b, c


def kernel(
    bo, kv_in, had, q_hbm, g_hbm, o_hbm,
    kg, vg, hand,
    q_v, g_v, o_v, kv, qr, qt, gr, gt, delta, qpos, m8, l8, lse, scores, ds_buf, pl_buf, dqt,
    rs_out, rs_in, total, fin, hs, zero_buf,
    loc_sem, ag_send, ag_recv, rs_send, rs_recv, h_send, h_recv,
):
    head_size = 128
    inv = np.float32(1.0 / math.sqrt(head_size))
    to_log2 = np.float32(math.log2(math.e) / math.sqrt(head_size))
    pipe = lax.axis_index("pipe")
    ctx = lax.axis_index("ctx")
    head = lax.axis_index("head")
    n_pipe = lax.axis_size("pipe")
    y = ctx // 2
    zh = ctx % 2

    def ring(step):
        return (pipe, ((y + step + NY) % NY) * 2 + zh, head)

    across = (pipe, y * 2 + (1 - zh), head)
    before = ((pipe + n_pipe - 1) % n_pipe, ctx, head)
    after = ((pipe + 1) % n_pipe, ctx, head)

    barrier = pltpu.get_barrier_semaphore()
    for other in (ring(1), ring(-1), across, before, after):
        pl.semaphore_signal(barrier, inc=1, device_id=other, device_id_type=MESH)

    loads = [
        pltpu.make_async_copy(src, dst, loc_sem.at[n])
        for n, (src, dst) in enumerate(((q_hbm, q_v), (g_hbm, g_v), (o_hbm, o_v)))
    ]
    for load in loads:
        load.start()

    for g in range(4):
        kv[ctx, g, 0] = (dot(kv_in[g, 0], had[...]) * inv).astype(BF16)
        kv[ctx, g, 1] = kv_in[g, 1]

    pl.semaphore_wait(barrier, 5)

    def block_of(half, i):
        sign = (1 - 2 * (i % 2)) * (1 - 2 * half)
        y_src = (y + sign * ((i + 1) // 2) + NY) % NY
        return y_src * 2 + (zh if half == 0 else 1 - zh)

    def ag_copy(pair, half, j, src, target):
        piece = kv.at[src, pl.ds(2 * pair, 2)]
        return pltpu.make_async_remote_copy(
            src_ref=piece, dst_ref=piece,
            send_sem=ag_send.at[pair, half, j], recv_sem=ag_recv.at[pair, half, j],
            device_id=target, device_id_type=MESH,
        )

    def z_copy(pair, src):
        piece = kv.at[src, pl.ds(2 * pair, 2)]
        return pltpu.make_async_remote_copy(
            src_ref=piece, dst_ref=piece,
            send_sem=ag_send.at[pair, 0, 0], recv_sem=ag_recv.at[pair, 1, 0],
            device_id=across, device_id_type=MESH,
        )

    def ag_event(e):
        pair, i = e // NY, e % NY
        for half in range(2):
            lead = 1 - 2 * half
            src = block_of(half, i)
            if half == 1:

                @pl.when(i == 0)
                def _():
                    z_copy(pair, src).wait_recv()

            @pl.when(i > 0)
            def _():
                ag_copy(pair, half, i, src, ring(1)).wait_recv()

            @pl.when(i == 0)
            def _():
                ag_copy(pair, half, 1, src, ring(lead)).start()
                ag_copy(pair, half, 2, src, ring(-lead)).start()

            @pl.when((i > 0) & (i <= 5))
            def _():
                way = lead * (2 * (i % 2) - 1)
                ag_copy(pair, half, i + 2, src, ring(way)).start()

    for pair in range(2):
        z_copy(pair, ctx).start()

    m8[...] = jnp.full(m8.shape, NEG, F32)
    l8[...] = jnp.zeros(l8.shape, F32)
    zero_buf[...] = jnp.zeros(zero_buf.shape, BF16)
    row = lax.broadcasted_iota(jnp.int32, qpos.shape, 1)
    starts = jnp.where(row < 512, bo[2 * ctx], bo[2 * ctx + 1])
    qpos[...] = starts * 64 + ((row >> 3) & 63)

    def prep(j, _):
        toks = pl.ds(pl.multiple_of(j * 16, 16), 16)
        rows = pl.ds(pl.multiple_of(j * 128, 128), 128)
        q_c = q_v[toks].astype(F32)
        g_c = g_v[toks].astype(F32)
        o_c = o_v[toks].astype(F32)
        for g in range(4):
            hd = slice(8 * g, 8 * g + 8)
            q_g = q_c[:, hd, :].reshape(128, 128).astype(BF16)
            rot = dot(q_g, had[...]) * inv
            qr[g, rows, :] = rot.astype(BF16)
            qt[g, :, rows] = rot.T.astype(BF16)
            g_g = g_c[:, hd, :].reshape(128, 128)
            o_g = o_c[:, hd, :].reshape(128, 128)
            gr[g, rows, :] = g_g.astype(BF16)
            gt[g, :, rows] = g_g.T.astype(BF16)
            sums = jnp.sum((g_g * o_g).T, axis=0, keepdims=True)
            delta[g, :, rows] = jnp.broadcast_to(sums, (8, 128))
        return 0

    ag_event(0)
    for load in loads:
        load.wait()
    lax.fori_loop(0, 8, prep, 0)
    lax.fori_loop(1, LOOK, lambda e, _: (ag_event(e), 0)[1], 0)

    place = (
        lax.broadcasted_iota(jnp.int32, (8, 8, CHUNK), 0) * 8
        + lax.broadcasted_iota(jnp.int32, (8, 8, CHUNK), 1)
    )

    def stat_unit(g, i):
        blocks = (block_of(0, i), block_of(1, i))
        k_two = jnp.concatenate([kv[blocks[0], g, 0], kv[blocks[1], g, 0]], axis=0)
        for c in range(1024 // CHUNK):
            cols = slice(c * CHUNK, (c + 1) * CHUNK)
            s = dot(k_two, qt[g, :, cols])
            q_at = qpos[:, cols]
            old = m8[g, :, cols]
            top = old
            parts = []
            for b in range(4):
                base = bo[2 * blocks[b // 2] + b % 2] * 64
                piece = s[64 * b : 64 * b + 64].reshape(8, 8, CHUNK) * to_log2
                piece = jnp.where(place <= (q_at - base)[None], piece, NEG)
                scores[g, blocks[b // 2], 64 * (b % 2) : 64 * (b % 2) + 64, cols] = piece.reshape(
                    64, CHUNK
                )
                top = jnp.maximum(top, jnp.max(piece, axis=0))
                parts.append(piece)
            run = l8[g, :, cols] * jnp.exp2(old - top)
            for piece in parts:
                run = run + jnp.sum(jnp.exp2(piece - top[None]), axis=0)
            m8[g, :, cols] = top
            l8[g, :, cols] = run

    def close_stats(g):
        top = jnp.max(m8[g], axis=0, keepdims=True)
        run = jnp.sum(l8[g] * jnp.exp2(m8[g] - top), axis=0, keepdims=True)
        lse[g] = jnp.broadcast_to(top + jnp.log2(run), (8, 1024))

    def rs_copy(g, j, target):
        return pltpu.make_async_remote_copy(
            src_ref=rs_out.at[g, j], dst_ref=rs_in.at[g, j],
            send_sem=rs_send.at[g, j], recv_sem=rs_recv.at[g, j],
            device_id=target, device_id_type=MESH,
        )

    def rs_z_copy(g):
        return pltpu.make_async_remote_copy(
            src_ref=rs_out.at[g, 7, :, pl.ds(0, 128)], dst_ref=rs_in.at[g, 7, :, pl.ds(0, 128)],
            send_sem=rs_send.at[g, 7], recv_sem=rs_recv.at[g, 7],
            device_id=across, device_id_type=MESH,
        )

    def hand_copy(g):
        return pltpu.make_async_remote_copy(
            src_ref=hs.at[g], dst_ref=hand.at[g],
            send_sem=h_send.at[g], recv_sem=h_recv.at[g],
            device_id=before, device_id_type=MESH,
        )

    def zero_copy(g):
        return pltpu.make_async_copy(zero_buf, hand.at[g], h_recv.at[g])

    def grad_unit(g, k, i):
        lead = 1 - 2 * k
        odd = i % 2
        sign = (2 * odd - 1) * lead
        y_dst = (y + sign * (4 - (i + 1) // 2) + NY) % NY
        first = 2 * y_dst
        k_two = jnp.concatenate([kv[first, g, 0], kv[first + 1, g, 0]], axis=0)
        v_two = jnp.concatenate([kv[first, g, 1], kv[first + 1, g, 1]], axis=0)

        @pl.when(i == 0)
        def _():
            close_stats(g)
            dqt[k] = jnp.zeros((128, 1024), F32)

        for c in range(1024 // CHUNK):
            cols = slice(c * CHUNK, (c + 1) * CHUNK)
            dp = dot(v_two, gt[g, :, cols]).reshape(2, 16, 8, CHUNK)
            s = scores[g, pl.ds(first, 2), :, cols].reshape(2, 16, 8, CHUNK)
            p = jnp.exp2(s - lse[g, :, cols][None, None])
            ds = p * (dp - delta[g, :, cols][None, None])
            ds = ds.reshape(256, CHUNK).astype(BF16)
            ds_buf[:, cols] = ds
            pl_buf[:, cols] = p.reshape(256, CHUNK).astype(BF16)
            dqt[k, :, cols] += lax.dot_general(
                k_two, ds, (((0,), (0,)), ((), ())), preferred_element_type=F32
            )
        total[0] = dot(ds_buf[...], qr[g])
        total[1] = dot(pl_buf[...], gr[g])

        @pl.when(i < 2)
        def _():
            rs_out[g, i] = total[...].astype(BF16)

        @pl.when((i >= 2) & (i < 7))
        def _():
            rs_copy(g, i - 2, ring(1)).wait_recv()
            rs_out[g, i] = (total[...] + rs_in[g, i - 2].astype(F32)).astype(BF16)

        @pl.when(i < 7)
        def _():
            rs_copy(g, i, ring(sign)).start()

        @pl.when(i == 7)
        def _():
            x = dqt[k] * inv
            a, b, c = split3(x)
            full = (dot(had[...], a) + dot(had[...], b) + dot(had[...], c)) * inv
            hs[g] = (full.T + gr[g].astype(F32)).astype(BF16)

            @pl.when(pipe > 0)
            def _():
                hand_copy(g).start()

            rs_copy(g, 5, ring(1)).wait_recv()
            rs_copy(g, 6, ring(1)).wait_recv()
            total[...] = total[...] + rs_in[g, 5].astype(F32) + rs_in[g, 6].astype(F32)
            theirs = pl.ds(pl.multiple_of((1 - zh) * 128, 128), 128)
            mine = pl.ds(pl.multiple_of(zh * 128, 128), 128)
            rs_out[g, 7, :, 0:128] = total[:, theirs].astype(BF16)
            rs_z_copy(g).start()
            fin[g] = total[:, mine]

    def finish(g):
        rs_z_copy(g).wait_recv()
        both = fin[g] + rs_in[g, 7, :, 0:128].astype(F32)
        a, b, c = split3(both[0] * inv)
        full = dot(a, had[...]) + dot(b, had[...]) + dot(c, had[...])
        kg[g] = (full * inv).astype(BF16)
        vg[g] = both[1].astype(BF16)

    def slot(t, _):
        turn, i = t // NY, t % NY

        @pl.when(t + LOOK < 2 * NY)
        def _():
            ag_event(t + LOOK)

        @pl.when(t < 2 * NY)
        def _():
            lax.fori_loop(0, 2, lambda k, _: (stat_unit(2 * turn + k, i), 0)[1], 0)

        @pl.when(t >= NY)
        def _():
            lax.fori_loop(0, 2, lambda k, _: (grad_unit(2 * turn - 2 + k, k, i), 0)[1], 0)

        return 0

    lax.fori_loop(0, 3 * NY, slot, 0)

    @pl.when(pipe == n_pipe - 1)
    def _():
        for g in range(4):
            zero_copy(g).start()

    for g in range(4):
        finish(g)

    @pl.when(pipe == n_pipe - 1)
    def _():
        for g in range(4):
            zero_copy(g).wait()

    @pl.when(pipe < n_pipe - 1)
    def _():
        for g in range(4):
            hand_copy(g).wait_recv()

    @pl.when(pipe > 0)
    def _():
        for g in range(4):
            hand_copy(g).wait_send()

    for pair in range(2):
        z_copy(pair, ctx).wait_send()
        for half in range(2):
            for j in range(1, 8):
                ag_copy(pair, half, j, ctx, ring(1)).wait_send()
    for g in range(4):
        for j in range(7):
            rs_copy(g, j, ring(1)).wait_send()
        rs_z_copy(g).wait_send()


def shards(queries, key_heads, value_heads, forward_out, output_grad, block_order):
    tok = queries.shape[1]
    kv_in = jnp.stack([key_heads[0], value_heads[0]]).transpose(2, 0, 1, 3)
    had = jnp.asarray(signs(128), BF16)
    vmem = pl.BlockSpec(memory_space=pltpu.VMEM)
    hbm = pl.BlockSpec(memory_space=pl.ANY)
    dma = pltpu.SemaphoreType.DMA
    kg, vg, hand = pl.pallas_call(
        kernel,
        out_shape=(
            jax.ShapeDtypeStruct((4, tok, 128), BF16),
            jax.ShapeDtypeStruct((4, tok, 128), BF16),
            jax.ShapeDtypeStruct((4, 8 * tok, 128), BF16),
        ),
        in_specs=[pl.BlockSpec(memory_space=pltpu.SMEM), vmem, vmem, hbm, hbm, hbm],
        out_specs=(vmem, vmem, hbm),
        scratch_shapes=[
            pltpu.VMEM((tok, 32, 128), BF16),
            pltpu.VMEM((tok, 32, 128), BF16),
            pltpu.VMEM((tok, 32, 128), BF16),
            pltpu.VMEM((16, 4, 2, 128, 128), BF16),
            pltpu.VMEM((4, 1024, 128), BF16),
            pltpu.VMEM((4, 128, 1024), BF16),
            pltpu.VMEM((4, 1024, 128), BF16),
            pltpu.VMEM((4, 128, 1024), BF16),
            pltpu.VMEM((4, 8, 1024), F32),
            pltpu.VMEM((8, 1024), jnp.int32),
            pltpu.VMEM((4, 8, 1024), F32),
            pltpu.VMEM((4, 8, 1024), F32),
            pltpu.VMEM((4, 8, 1024), F32),
            pltpu.VMEM((4, 16, 128, 1024), F32),
            pltpu.VMEM((256, 1024), BF16),
            pltpu.VMEM((256, 1024), BF16),
            pltpu.VMEM((2, 128, 1024), F32),
            pltpu.VMEM((4, 8, 2, 256, 128), BF16),
            pltpu.VMEM((4, 8, 2, 256, 128), BF16),
            pltpu.VMEM((2, 256, 128), F32),
            pltpu.VMEM((4, 2, 128, 128), F32),
            pltpu.VMEM((4, 1024, 128), BF16),
            pltpu.VMEM((1024, 128), BF16),
            dma((3,)),
            dma((2, 2, 8)),
            dma((2, 2, 8)),
            dma((4, 8)),
            dma((4, 8)),
            dma((4,)),
            dma((4,)),
        ],
        compiler_params=pltpu.CompilerParams(
            collective_id=0, has_side_effects=True, vmem_limit_bytes=60 * 1024 * 1024
        ),
        cost_estimate=pl.CostEstimate(
            flops=11_000_000_000, bytes_accessed=5_000_000, transcendentals=17_000_000
        ),
    )(block_order, kv_in, had, queries[0], output_grad[0], forward_out[0])
    key_grad = kg.transpose(1, 0, 2)[None]
    value_grad = vg.transpose(1, 0, 2)[None]
    handed = hand.reshape(4, tok, 8, 128).transpose(1, 0, 2, 3).reshape(1, tok, 32, 128)
    return (key_grad, value_grad, handed)


def solution(mesh):
    placed = P("pipe", "ctx", "head", None)
    return jax.shard_map(
        shards,
        mesh=mesh,
        in_specs=(placed,) * 5 + (P(),),
        out_specs=(placed,) * 3,
        check_vma=False,
    )
```

```python
import math

import jax
import jax.numpy as jnp
import numpy as np
from jax import lax
from jax.experimental import pallas as pl
from jax.experimental.pallas import tpu as pltpu
from jax.sharding import PartitionSpec as P

MESH = pl.DeviceIdType.MESH
NEG = -1e30
F32 = jnp.float32
BF16 = jnp.bfloat16
NY = 8
ROWS_AT = 4
REST = 8 - 2 * (NY - ROWS_AT - 2)
LAG = 2
AHEAD = LAG + 2
Z_STEPS = (None, None, 3)
CHUNK = 512


def signs(size):
    index = np.arange(size)
    ands = index[:, None] & index[None, :]
    parity = np.zeros((size, size), np.int64)
    for bit in range(size.bit_length() - 1):
        parity ^= (ands >> bit) & 1
    return 1.0 - 2.0 * parity


def dot(a, b):
    return jnp.dot(a, b, preferred_element_type=F32)


def split3(x):
    a = x.astype(BF16)
    r = x - a.astype(F32)
    b = r.astype(BF16)
    c = (r - b.astype(F32)).astype(BF16)
    return a, b, c


def kernel(
    bo, kv_in, had, q_hbm, g_hbm, o_hbm,
    kg, vg, hand,
    q_v, g_v, o_v, kv, qr, qt, gr, gt, delta, qpos, m8, l8, lse, scores, ds_buf, pl_buf, dqt,
    rs_out, rs_in, part, total, fin, hs, zero_buf,
    loc_sem, row_send, row_recv, ag_send, ag_recv, rs_send, rs_recv, h_send, h_recv,
):
    head_size = 128
    inv = np.float32(1.0 / math.sqrt(head_size))
    to_log2 = np.float32(math.log2(math.e) / math.sqrt(head_size))
    pipe = lax.axis_index("pipe")
    ctx = lax.axis_index("ctx")
    head = lax.axis_index("head")
    n_pipe = lax.axis_size("pipe")
    y = ctx // 2
    zh = ctx % 2

    def ring(step):
        return (pipe, ((y + step + NY) % NY) * 2 + zh, head)

    across = (pipe, y * 2 + (1 - zh), head)
    mate = y * 2 + (1 - zh)
    split_g = 2 + zh
    other_g = 3 - zh
    prev, following = (pipe + n_pipe - 1) % n_pipe, (pipe + 1) % n_pipe
    before, before_mate = (prev, ctx, head), (prev, mate, head)
    after, after_mate = (following, ctx, head), (following, mate, head)

    barrier = pltpu.get_barrier_semaphore()
    for other in (ring(1), ring(-1), across, before, after, before_mate, after_mate):
        pl.semaphore_signal(barrier, inc=1, device_id=other, device_id_type=MESH)

    loads = [
        pltpu.make_async_copy(src, dst, loc_sem.at[n])
        for n, (src, dst) in enumerate(((q_hbm, q_v), (g_hbm, g_v), (o_hbm, o_v)))
    ]
    for load in loads:
        load.start()

    for g in range(4):
        kv[ctx, g, 0] = (dot(kv_in[g, 0], had[...]) * inv).astype(BF16)
        kv[ctx, g, 1] = kv_in[g, 1]

    pl.semaphore_wait(barrier, 7)

    def block_of(half, i):
        sign = (1 - 2 * (i % 2)) * (1 - 2 * half)
        y_src = (y + sign * ((i + 1) // 2) + NY) % NY
        return y_src * 2 + (zh if half == 0 else 1 - zh)

    def kv_group(rg):
        return jnp.where(rg < 2, rg, split_g)

    def ag_copy(g, half, j, src, target):
        piece = kv.at[src, kv_group(g)]
        return pltpu.make_async_remote_copy(
            src_ref=piece, dst_ref=piece,
            send_sem=ag_send.at[g, half, j], recv_sem=ag_recv.at[g, half, j],
            device_id=target, device_id_type=MESH,
        )

    def z_copy(g, src):
        piece = kv.at[src, other_g if g == 2 else g]
        return pltpu.make_async_remote_copy(
            src_ref=piece, dst_ref=piece,
            send_sem=ag_send.at[g, 0, 0], recv_sem=ag_recv.at[g, 1, 0],
            device_id=across, device_id_type=MESH,
        )

    def ag_z(g):
        piece = kv.at[ctx, g]
        return pltpu.make_async_remote_copy(
            src_ref=piece, dst_ref=piece,
            send_sem=ag_send.at[g, 0, 0], recv_sem=ag_recv.at[g, 1, 0],
            device_id=across, device_id_type=MESH,
        )

    def row_copies():
        return [
            pltpu.make_async_remote_copy(
                src_ref=ref.at[4], dst_ref=ref.at[3],
                send_sem=row_send.at[n], recv_sem=row_recv.at[n],
                device_id=across, device_id_type=MESH,
            )
            for n, ref in enumerate((qr, gr, delta))
        ]

    def ag_event(half, e):
        pair, i = e // NY, e % NY
        lead = 1 - 2 * half
        src = block_of(half, i)

        def one(k, _):
            g = 2 * pair + k
            if half == 1:

                @pl.when(i == 0)
                def _():
                    ag_z(g).wait_recv()

            @pl.when(i > 0)
            def _():
                ag_copy(g, half, i, src, ring(1)).wait_recv()

            @pl.when(i == 0)
            def _():
                ag_copy(g, half, 1, src, ring(lead)).start()
                ag_copy(g, half, 2, src, ring(-lead)).start()

            @pl.when((i > 0) & (i <= 5))
            def _():
                way = lead * (2 * (i % 2) - 1)
                ag_copy(g, half, i + 2, src, ring(way)).start()

            return 0

        lax.fori_loop(0, 2 - pair, one, 0)

    def ag_step(u):
        @pl.when(u < 2 * NY)
        def _():
            ag_event(0, u)

        @pl.when((u >= LAG) & (u < LAG + 2 * NY))
        def _():
            ag_event(1, u - LAG)

        for g, when in enumerate(Z_STEPS):
            if when is not None:

                @pl.when(u == when)
                def _():
                    z_copy(g, ctx).start()

    for g, when in enumerate(Z_STEPS):
        if when is None:
            z_copy(g, ctx).start()

    m8[...] = jnp.full(m8.shape, NEG, F32)
    l8[...] = jnp.zeros(l8.shape, F32)
    zero_buf[...] = jnp.zeros(zero_buf.shape, BF16)
    row = lax.broadcasted_iota(jnp.int32, (8, 1024), 1)
    for n, block in enumerate((ctx, mate)):
        starts = jnp.where(row < 512, bo[2 * block], bo[2 * block + 1])
        qpos[n] = starts * 64 + ((row >> 3) & 63)

    def prep(j, _):
        toks = pl.ds(pl.multiple_of(j * 16, 16), 16)
        rows = pl.ds(pl.multiple_of(j * 128, 128), 128)
        q_c = q_v[toks].astype(F32)
        g_c = g_v[toks].astype(F32)
        o_c = o_v[toks].astype(F32)
        for g in range(4):
            hd = slice(8 * g, 8 * g + 8)
            to = g if g < 2 else jnp.where(g == split_g, 2, 4)
            q_g = q_c[:, hd, :].reshape(128, 128).astype(BF16)
            rot = dot(q_g, had[...]) * inv
            qr[to, rows, :] = rot.astype(BF16)
            qt[to, :, rows] = rot.T.astype(BF16)
            g_g = g_c[:, hd, :].reshape(128, 128)
            o_g = o_c[:, hd, :].reshape(128, 128)
            gr[to, rows, :] = g_g.astype(BF16)
            gt[to, :, rows] = g_g.T.astype(BF16)
            sums = jnp.sum((g_g * o_g).T, axis=0, keepdims=True)
            delta[to, :, rows] = jnp.broadcast_to(sums, (8, 128))
        return 0

    def warm(j, _):
        @pl.when(j < AHEAD)
        def _():
            ag_step(j)

        @pl.when(j == 0)
        def _():
            for load in loads:
                load.wait()

        prep(j, 0)
        return 0

    lax.fori_loop(0, 8, warm, 0)
    for copy in row_copies():
        copy.start()

    def take_rows():
        for copy in row_copies():
            copy.wait_recv()

        def turned(j, _):
            rows = pl.ds(pl.multiple_of(j * 128, 128), 128)
            qt[3, :, rows] = qr[3, rows, :].astype(F32).T.astype(BF16)
            gt[3, :, rows] = gr[3, rows, :].astype(F32).T.astype(BF16)
            return 0

        lax.fori_loop(0, 8, turned, 0)

    place = (
        lax.broadcasted_iota(jnp.int32, (8, 8, CHUNK), 0) * 8
        + lax.broadcasted_iota(jnp.int32, (8, 8, CHUNK), 1)
    )

    def stat_unit(g, i):
        blocks = (block_of(0, i), block_of(1, i))
        kg_at = kv_group(g)
        side = jnp.where(g == 3, 1, 0)
        k_two = jnp.concatenate([kv[blocks[0], kg_at, 0], kv[blocks[1], kg_at, 0]], axis=0)
        for c in range(1024 // CHUNK):
            cols = slice(c * CHUNK, (c + 1) * CHUNK)
            s = dot(k_two, qt[g, :, cols])
            q_at = qpos[side, :, cols]
            old = m8[g, :, cols]
            top = old
            parts = []
            for b in range(4):
                base = bo[2 * blocks[b // 2] + b % 2] * 64
                piece = s[64 * b : 64 * b + 64].reshape(8, 8, CHUNK) * to_log2
                piece = jnp.where(place <= (q_at - base)[None], piece, NEG)
                scores[g, blocks[b // 2], 64 * (b % 2) : 64 * (b % 2) + 64, cols] = piece.reshape(
                    64, CHUNK
                )
                top = jnp.maximum(top, jnp.max(piece, axis=0))
                parts.append(piece)
            run = l8[g, :, cols] * jnp.exp2(old - top)
            for piece in parts:
                run = run + jnp.sum(jnp.exp2(piece - top[None]), axis=0)
            m8[g, :, cols] = top
            l8[g, :, cols] = run

    def close_stats(g):
        top = jnp.max(m8[g], axis=0, keepdims=True)
        run = jnp.sum(l8[g] * jnp.exp2(m8[g] - top), axis=0, keepdims=True)
        lse[g] = jnp.broadcast_to(top + jnp.log2(run), (8, 1024))

    def rs_copy(g, j, d, target):
        return pltpu.make_async_remote_copy(
            src_ref=rs_out.at[g, j, d], dst_ref=rs_in.at[g, j, d],
            send_sem=rs_send.at[g, j, d], recv_sem=rs_recv.at[g, j, d],
            device_id=target, device_id_type=MESH,
        )

    def rs_z_copy(g):
        return pltpu.make_async_remote_copy(
            src_ref=rs_out.at[g, 7, :, pl.ds(0, 128)], dst_ref=rs_in.at[g, 7, :, pl.ds(0, 128)],
            send_sem=rs_send.at[g, 7, 0], recv_sem=rs_recv.at[g, 7, 0],
            device_id=across, device_id_type=MESH,
        )

    def hand_copy(g):
        return pltpu.make_async_remote_copy(
            src_ref=hs.at[g], dst_ref=hand.at[kv_group(g)],
            send_sem=h_send.at[g], recv_sem=h_recv.at[g],
            device_id=(prev, jnp.where(g == 3, mate, ctx), head), device_id_type=MESH,
        )

    def zero_copy(g):
        return pltpu.make_async_copy(zero_buf, hand.at[g], h_recv.at[g])

    def grad_unit(g, i):
        lead = jnp.where(g == 1, -1, 1)
        kg_at = kv_group(g)
        odd = i % 2
        sign = (2 * odd - 1) * lead
        y_dst = (y + sign * (4 - (i + 1) // 2) + NY) % NY
        first = 2 * y_dst
        k_two = jnp.concatenate([kv[first, kg_at, 0], kv[first + 1, kg_at, 0]], axis=0)
        v_two = jnp.concatenate([kv[first, kg_at, 1], kv[first + 1, kg_at, 1]], axis=0)

        k_t = k_two.T

        @pl.when(i == 0)
        def _():
            close_stats(g)
            dqt[g] = jnp.zeros((128, 1024), F32)

        for c in range(1024 // CHUNK):
            cols = slice(c * CHUNK, (c + 1) * CHUNK)
            dp = dot(v_two, gt[g, :, cols]).reshape(2, 16, 8, CHUNK)
            s = scores[g, pl.ds(first, 2), :, cols].reshape(2, 16, 8, CHUNK)
            p = jnp.exp2(s - lse[g, :, cols][None, None])
            ds = p * (dp - delta[g, :, cols][None, None])
            ds = ds.reshape(256, CHUNK).astype(BF16)
            ds_buf[:, cols] = ds
            pl_buf[:, cols] = p.reshape(256, CHUNK).astype(BF16)
        dqt[g] += dot(k_t, ds_buf[...])
        total[0] = dot(ds_buf[...], qr[g])
        total[1] = dot(pl_buf[...], gr[g])

        @pl.when(i == 7)
        def _():
            x = dqt[g] * inv
            a, b, c = split3(x)
            full = (dot(had[...], a) + dot(had[...], b) + dot(had[...], c)) * inv
            hs[g] = (full.T + gr[g].astype(F32)).astype(BF16)

            @pl.when(pipe > 0)
            def _():
                hand_copy(g).start()

        @pl.when(g == 3)
        def _():
            part[i] = total[...]

        @pl.when(g == 2)
        def _():
            total[...] += part[i]

        @pl.when(g < 3)
        def _():
            send_sums(g, i, sign)

    def send_sums(g, i, sign):
        for d in range(2):

            @pl.when(i < 2)
            def _():
                rs_out[g, i, d] = total[d].astype(BF16)

            @pl.when((i >= 2) & (i < 7))
            def _():
                rs_copy(g, i - 2, d, ring(1)).wait_recv()
                rs_out[g, i, d] = (total[d] + rs_in[g, i - 2, d].astype(F32)).astype(BF16)

            @pl.when(i < 7)
            def _():
                rs_copy(g, i, d, ring(sign)).start()

        @pl.when(i == 7)
        def _():
            for d in range(2):
                for j in (5, 6):
                    rs_copy(g, j, d, ring(1)).wait_recv()
            total[...] = total[...] + rs_in[g, 5].astype(F32) + rs_in[g, 6].astype(F32)
            theirs = pl.ds(pl.multiple_of((1 - zh) * 128, 128), 128)
            mine = pl.ds(pl.multiple_of(zh * 128, 128), 128)
            rs_out[g, 7, :, 0:128] = total[:, theirs].astype(BF16)
            rs_z_copy(g).start()
            fin[g] = total[:, mine]

    def put(g, both):
        a, b, c = split3(both[0] * inv)
        full = dot(a, had[...]) + dot(b, had[...]) + dot(c, had[...])
        kg[g] = (full * inv).astype(BF16)
        vg[g] = both[1].astype(BF16)

    def finish(g):
        rs_z_copy(g).wait_recv()
        theirs = rs_in[g, 7, :, 0:128].astype(F32)
        if g < 2:
            put(g, fin[g] + theirs)
        else:
            put(split_g, fin[g])
            put(other_g, theirs)

    def slot(t, _):
        turn, i = t // NY, t % NY

        ag_step(t + AHEAD)

        def stat(g, at):
            stat_unit(g, at)
            return 0

        @pl.when(turn == 0)
        def _():
            lax.fori_loop(0, 2, lambda k, _: stat(k, i), 0)

        @pl.when((turn == 1) & (i == ROWS_AT))
        def _():
            take_rows()

        @pl.when(turn == 1)
        def _():
            late = i - ROWS_AT
            many = jnp.where((late >= 0) & (late < 2), 5, 1)
            lax.fori_loop(
                0, many,
                lambda k, _: stat(jnp.where(k == 0, 2, 3), jnp.where(k == 0, i, 4 * late + k - 1)),
                0,
            )

        @pl.when(turn > 0)
        def _():
            early = i - (ROWS_AT + 2)
            many = jnp.where(
                turn == 1, jnp.where(early >= 0, 3, 1), jnp.where(i < REST, 3, 2)
            )

            def one(k, _):
                g = jnp.where(turn == 1, jnp.where(k == 0, 0, 3), 1 + k)
                at = jnp.where(
                    turn == 1,
                    jnp.where(k == 0, i, 2 * early + k - 1),
                    jnp.where(k == 2, NY - REST + i, i),
                )
                grad_unit(g, at)
                return 0

            lax.fori_loop(0, many, one, 0)

        @pl.when(t == 2 * NY + 2)
        def _():
            finish(0)

        return 0

    lax.fori_loop(0, 3 * NY, slot, 0)

    @pl.when(pipe == n_pipe - 1)
    def _():
        for g in range(4):
            zero_copy(g).start()

    for g in range(1, 3):
        finish(g)

    @pl.when(pipe == n_pipe - 1)
    def _():
        for g in range(4):
            zero_copy(g).wait()

    @pl.when(pipe < n_pipe - 1)
    def _():
        for g in range(4):
            hand_copy(g).wait_recv()

    @pl.when(pipe > 0)
    def _():
        for g in range(4):
            hand_copy(g).wait_send()

    for copy in row_copies():
        copy.wait_send()
    for g in range(3):
        z_copy(g, ctx).wait_send()
        for half in range(2):
            for j in range(1, 8):
                ag_copy(g, half, j, ctx, ring(1)).wait_send()
        for j in range(7):
            for d in range(2):
                rs_copy(g, j, d, ring(1)).wait_send()
        rs_z_copy(g).wait_send()


def shards(queries, key_heads, value_heads, forward_out, output_grad, block_order):
    tok = queries.shape[1]
    kv_in = jnp.stack([key_heads[0], value_heads[0]]).transpose(2, 0, 1, 3)
    had = jnp.asarray(signs(128), BF16)
    vmem = pl.BlockSpec(memory_space=pltpu.VMEM)
    hbm = pl.BlockSpec(memory_space=pl.ANY)
    dma = pltpu.SemaphoreType.DMA
    kg, vg, hand = pl.pallas_call(
        kernel,
        out_shape=(
            jax.ShapeDtypeStruct((4, tok, 128), BF16),
            jax.ShapeDtypeStruct((4, tok, 128), BF16),
            jax.ShapeDtypeStruct((4, 8 * tok, 128), BF16),
        ),
        in_specs=[pl.BlockSpec(memory_space=pltpu.SMEM), vmem, vmem, hbm, hbm, hbm],
        out_specs=(vmem, vmem, hbm),
        scratch_shapes=[
            pltpu.VMEM((tok, 32, 128), BF16),
            pltpu.VMEM((tok, 32, 128), BF16),
            pltpu.VMEM((tok, 32, 128), BF16),
            pltpu.VMEM((16, 4, 2, 128, 128), BF16),
            pltpu.VMEM((5, 1024, 128), BF16),
            pltpu.VMEM((5, 128, 1024), BF16),
            pltpu.VMEM((5, 1024, 128), BF16),
            pltpu.VMEM((5, 128, 1024), BF16),
            pltpu.VMEM((5, 8, 1024), F32),
            pltpu.VMEM((2, 8, 1024), jnp.int32),
            pltpu.VMEM((4, 8, 1024), F32),
            pltpu.VMEM((4, 8, 1024), F32),
            pltpu.VMEM((4, 8, 1024), F32),
            pltpu.VMEM((4, 16, 128, 1024), F32),
            pltpu.VMEM((256, 1024), BF16),
            pltpu.VMEM((256, 1024), BF16),
            pltpu.VMEM((4, 128, 1024), F32),
            pltpu.VMEM((3, 8, 2, 256, 128), BF16),
            pltpu.VMEM((3, 8, 2, 256, 128), BF16),
            pltpu.VMEM((8, 2, 256, 128), F32),
            pltpu.VMEM((2, 256, 128), F32),
            pltpu.VMEM((3, 2, 128, 128), F32),
            pltpu.VMEM((4, 1024, 128), BF16),
            pltpu.VMEM((1024, 128), BF16),
            dma((3,)),
            dma((3,)),
            dma((3,)),
            dma((3, 2, 8)),
            dma((3, 2, 8)),
            dma((3, 8, 2)),
            dma((3, 8, 2)),
            dma((4,)),
            dma((4,)),
        ],
        compiler_params=pltpu.CompilerParams(
            collective_id=0, has_side_effects=True, vmem_limit_bytes=60 * 1024 * 1024
        ),
        cost_estimate=pl.CostEstimate(
            flops=11_000_000_000, bytes_accessed=5_000_000, transcendentals=17_000_000
        ),
    )(block_order, kv_in, had, queries[0], output_grad[0], forward_out[0])
    key_grad = kg.transpose(1, 0, 2)[None]
    value_grad = vg.transpose(1, 0, 2)[None]
    handed = hand.reshape(4, tok, 8, 128).transpose(1, 0, 2, 3).reshape(1, tok, 32, 128)
    return (key_grad, value_grad, handed)


def solution(mesh):
    placed = P("pipe", "ctx", "head", None)
    return jax.shard_map(
        shards,
        mesh=mesh,
        in_specs=(placed,) * 5 + (P(),),
        out_specs=(placed,) * 3,
        check_vma=False,
    )
```

```python
import math

import jax
import jax.numpy as jnp
import numpy as np
from jax import lax
from jax.experimental import pallas as pl
from jax.experimental.pallas import tpu as pltpu
from jax.sharding import PartitionSpec as P

MESH = pl.DeviceIdType.MESH
NEG = -1e30
F32 = jnp.float32
BF16 = jnp.bfloat16
NY = 8
ROWS_AT = 4
REST = 8 - 2 * (NY - ROWS_AT - 2)
LAG = 1
AHEAD = LAG + 3
Z_STEPS = (None, None, 2)
CHUNK = 512


def signs(size):
    index = np.arange(size)
    ands = index[:, None] & index[None, :]
    parity = np.zeros((size, size), np.int64)
    for bit in range(size.bit_length() - 1):
        parity ^= (ands >> bit) & 1
    return 1.0 - 2.0 * parity


def dot(a, b):
    return jnp.dot(a, b, preferred_element_type=F32)


def split3(x):
    a = x.astype(BF16)
    r = x - a.astype(F32)
    b = r.astype(BF16)
    c = (r - b.astype(F32)).astype(BF16)
    return a, b, c


def kernel(
    bo, k_in, v_in, had, q_hbm, g_hbm, o_hbm,
    kg, vg, hand,
    q_v, g_v, o_v, kv, qr, qt, gr, gt, delta, qpos, m8, l8, lse, scores, ds_buf, pl_buf, dqt,
    rs_out, rs_in, part, total, fin, hs, zero_buf,
    loc_sem, row_send, row_recv, ag_send, ag_recv, rs_send, rs_recv, h_send, h_recv,
):
    head_size = 128
    inv = np.float32(1.0 / math.sqrt(head_size))
    to_log2 = np.float32(math.log2(math.e) / math.sqrt(head_size))
    pipe = lax.axis_index("pipe")
    ctx = lax.axis_index("ctx")
    head = lax.axis_index("head")
    n_pipe = lax.axis_size("pipe")
    y = ctx // 2
    zh = ctx % 2

    def ring(step):
        return (pipe, ((y + step + NY) % NY) * 2 + zh, head)

    across = (pipe, y * 2 + (1 - zh), head)
    mate = y * 2 + (1 - zh)
    split_g = 2 + zh
    other_g = 3 - zh
    prev, following = (pipe + n_pipe - 1) % n_pipe, (pipe + 1) % n_pipe
    before, before_mate = (prev, ctx, head), (prev, mate, head)
    after, after_mate = (following, ctx, head), (following, mate, head)

    barrier = pltpu.get_barrier_semaphore()
    for other in (ring(1), ring(-1), across, before, after, before_mate, after_mate):
        pl.semaphore_signal(barrier, inc=1, device_id=other, device_id_type=MESH)

    loads = [
        pltpu.make_async_copy(src, dst, loc_sem.at[n])
        for n, (src, dst) in enumerate(((q_hbm, q_v), (g_hbm, g_v), (o_hbm, o_v)))
    ]
    for load in loads:
        load.start()

    for g in range(4):
        kv[ctx, g, 0] = (dot(k_in[g], had[...]) * inv).astype(BF16)
        kv[ctx, g, 1] = v_in[g]

    pl.semaphore_wait(barrier, 7)

    def block_of(half, i):
        sign = (1 - 2 * (i % 2)) * (1 - 2 * half)
        y_src = (y + sign * ((i + 1) // 2) + NY) % NY
        return y_src * 2 + (zh if half == 0 else 1 - zh)

    def kv_group(rg):
        return jnp.where(rg < 2, rg, split_g)

    def ag_copy(g, half, j, src, target):
        piece = kv.at[src, kv_group(g)]
        return pltpu.make_async_remote_copy(
            src_ref=piece, dst_ref=piece,
            send_sem=ag_send.at[g, half, j], recv_sem=ag_recv.at[g, half, j],
            device_id=target, device_id_type=MESH,
        )

    def z_copy(g, src):
        piece = kv.at[src, other_g if g == 2 else g]
        return pltpu.make_async_remote_copy(
            src_ref=piece, dst_ref=piece,
            send_sem=ag_send.at[g, 0, 0], recv_sem=ag_recv.at[g, 1, 0],
            device_id=across, device_id_type=MESH,
        )

    def ag_z(g):
        piece = kv.at[ctx, g]
        return pltpu.make_async_remote_copy(
            src_ref=piece, dst_ref=piece,
            send_sem=ag_send.at[g, 0, 0], recv_sem=ag_recv.at[g, 1, 0],
            device_id=across, device_id_type=MESH,
        )

    def row_copies():
        return [
            pltpu.make_async_remote_copy(
                src_ref=ref.at[4], dst_ref=ref.at[3],
                send_sem=row_send.at[n], recv_sem=row_recv.at[n],
                device_id=across, device_id_type=MESH,
            )
            for n, ref in enumerate((qr, gr, delta))
        ]

    def ag_event(half, e):
        pair, i = e // NY, e % NY
        lead = 1 - 2 * half
        src = block_of(half, i)

        def one(k, _):
            g = 2 * pair + k
            if half == 1:

                @pl.when(i == 0)
                def _():
                    ag_z(g).wait_recv()

            @pl.when(i > 0)
            def _():
                ag_copy(g, half, i, src, ring(1)).wait_recv()

            @pl.when(i == 0)
            def _():
                ag_copy(g, half, 1, src, ring(lead)).start()
                ag_copy(g, half, 2, src, ring(-lead)).start()

            @pl.when((i > 0) & (i <= 5))
            def _():
                way = lead * (2 * (i % 2) - 1)
                ag_copy(g, half, i + 2, src, ring(way)).start()

            return 0

        lax.fori_loop(0, 2 - pair, one, 0)

    def ag_mate(u):
        @pl.when((u >= LAG) & (u < LAG + 2 * NY))
        def _():
            ag_event(1, u - LAG)

    def ag_own(u):
        @pl.when(u < 2 * NY)
        def _():
            ag_event(0, u)

        for g, when in enumerate(Z_STEPS):
            if when is not None:

                @pl.when(u == when)
                def _():
                    z_copy(g, ctx).start()

    for g, when in enumerate(Z_STEPS):
        if when is None:
            z_copy(g, ctx).start()

    m8[...] = jnp.full(m8.shape, NEG, F32)
    l8[...] = jnp.zeros(l8.shape, F32)
    zero_buf[...] = jnp.zeros(zero_buf.shape, BF16)
    row = lax.broadcasted_iota(jnp.int32, (8, 1024), 1)
    for n, block in enumerate((ctx, mate)):
        starts = jnp.where(row < 512, bo[2 * block], bo[2 * block + 1])
        qpos[n] = starts * 64 + ((row >> 3) & 63)

    def prep(j, _):
        toks = pl.ds(pl.multiple_of(j * 16, 16), 16)
        rows = pl.ds(pl.multiple_of(j * 128, 128), 128)
        q_c = q_v[toks].astype(F32)
        g_c = g_v[toks].astype(F32)
        o_c = o_v[toks].astype(F32)
        for g in range(4):
            hd = slice(8 * g, 8 * g + 8)
            to = g if g < 2 else jnp.where(g == split_g, 2, 4)
            q_g = q_c[:, hd, :].reshape(128, 128).astype(BF16)
            rot = dot(q_g, had[...]) * inv
            qr[to, rows, :] = rot.astype(BF16)
            qt[to, :, rows] = rot.T.astype(BF16)
            g_g = g_c[:, hd, :].reshape(128, 128)
            o_g = o_c[:, hd, :].reshape(128, 128)
            gr[to, rows, :] = g_g.astype(BF16)
            gt[to, :, rows] = g_g.T.astype(BF16)
            sums = jnp.sum((g_g * o_g).T, axis=0, keepdims=True)
            delta[to, :, rows] = jnp.broadcast_to(sums, (8, 128))
        return 0

    def warm(j, _):
        @pl.when(j < AHEAD)
        def _():
            ag_own(j)
            ag_mate(j)

        @pl.when(j == 0)
        def _():
            for load in loads:
                load.wait()

        prep(j, 0)
        return 0

    lax.fori_loop(0, 8, warm, 0)
    for copy in row_copies():
        copy.start()

    def take_rows():
        for copy in row_copies():
            copy.wait_recv()

        def turned(j, _):
            rows = pl.ds(pl.multiple_of(j * 128, 128), 128)
            qt[3, :, rows] = qr[3, rows, :].astype(F32).T.astype(BF16)
            gt[3, :, rows] = gr[3, rows, :].astype(F32).T.astype(BF16)
            return 0

        lax.fori_loop(0, 8, turned, 0)

    place = (
        lax.broadcasted_iota(jnp.int32, (8, 8, CHUNK), 0) * 8
        + lax.broadcasted_iota(jnp.int32, (8, 8, CHUNK), 1)
    )

    def stat_unit(g, i):
        blocks = (block_of(0, i), block_of(1, i))
        kg_at = kv_group(g)
        side = jnp.where(g == 3, 1, 0)
        k_two = jnp.concatenate([kv[blocks[0], kg_at, 0], kv[blocks[1], kg_at, 0]], axis=0)
        for c in range(1024 // CHUNK):
            cols = slice(c * CHUNK, (c + 1) * CHUNK)
            s = dot(k_two, qt[g, :, cols])
            q_at = qpos[side, :, cols]
            old = m8[g, :, cols]
            top = old
            parts = []
            for b in range(4):
                base = bo[2 * blocks[b // 2] + b % 2] * 64
                piece = s[64 * b : 64 * b + 64].reshape(8, 8, CHUNK) * to_log2
                piece = jnp.where(place <= (q_at - base)[None], piece, NEG)
                scores[g, blocks[b // 2], 64 * (b % 2) : 64 * (b % 2) + 64, cols] = piece.reshape(
                    64, CHUNK
                )
                top = jnp.maximum(top, jnp.max(piece, axis=0))
                parts.append(piece)
            run = l8[g, :, cols] * jnp.exp2(old - top)
            for piece in parts:
                run = run + jnp.sum(jnp.exp2(piece - top[None]), axis=0)
            m8[g, :, cols] = top
            l8[g, :, cols] = run

    def close_stats(g):
        top = jnp.max(m8[g], axis=0, keepdims=True)
        run = jnp.sum(l8[g] * jnp.exp2(m8[g] - top), axis=0, keepdims=True)
        lse[g] = jnp.broadcast_to(top + jnp.log2(run), (8, 1024))

    def rs_copy(g, j, d, target):
        return pltpu.make_async_remote_copy(
            src_ref=rs_out.at[g, j, d], dst_ref=rs_in.at[g, j, d],
            send_sem=rs_send.at[g, j, d], recv_sem=rs_recv.at[g, j, d],
            device_id=target, device_id_type=MESH,
        )

    def rs_z_copy(g):
        return pltpu.make_async_remote_copy(
            src_ref=rs_out.at[g, 7, :, pl.ds(0, 128)], dst_ref=rs_in.at[g, 7, :, pl.ds(0, 128)],
            send_sem=rs_send.at[g, 7, 0], recv_sem=rs_recv.at[g, 7, 0],
            device_id=across, device_id_type=MESH,
        )

    def hand_copy(g):
        return pltpu.make_async_remote_copy(
            src_ref=hs.at[g], dst_ref=hand.at[kv_group(g)],
            send_sem=h_send.at[g], recv_sem=h_recv.at[g],
            device_id=(prev, jnp.where(g == 3, mate, ctx), head), device_id_type=MESH,
        )

    def zero_copy(g):
        return pltpu.make_async_copy(zero_buf, hand.at[g], h_recv.at[g])

    def grad_unit(g, i):
        lead = jnp.where(g == 1, -1, 1)
        kg_at = kv_group(g)
        odd = i % 2
        sign = (2 * odd - 1) * lead
        y_dst = (y + sign * (4 - (i + 1) // 2) + NY) % NY
        first = 2 * y_dst
        k_two = jnp.concatenate([kv[first, kg_at, 0], kv[first + 1, kg_at, 0]], axis=0)
        v_two = jnp.concatenate([kv[first, kg_at, 1], kv[first + 1, kg_at, 1]], axis=0)

        k_t = k_two.T

        @pl.when(i == 0)
        def _():
            close_stats(g)
            dqt[g] = jnp.zeros((128, 1024), F32)

        for c in range(1024 // CHUNK):
            cols = slice(c * CHUNK, (c + 1) * CHUNK)
            dp = dot(v_two, gt[g, :, cols]).reshape(2, 16, 8, CHUNK)
            s = scores[g, pl.ds(first, 2), :, cols].reshape(2, 16, 8, CHUNK)
            p = jnp.exp2(s - lse[g, :, cols][None, None])
            ds = p * (dp - delta[g, :, cols][None, None])
            ds = ds.reshape(256, CHUNK).astype(BF16)
            ds_buf[:, cols] = ds
            pl_buf[:, cols] = p.reshape(256, CHUNK).astype(BF16)
        dqt[g] += dot(k_t, ds_buf[...])
        total[0] = dot(ds_buf[...], qr[g])
        total[1] = dot(pl_buf[...], gr[g])

        @pl.when(i == 7)
        def _():
            x = dqt[g] * inv
            a, b, c = split3(x)
            full = (dot(had[...], a) + dot(had[...], b) + dot(had[...], c)) * inv
            hs[g] = (full.T + gr[g].astype(F32)).astype(BF16)

            @pl.when(pipe > 0)
            def _():
                hand_copy(g).start()

        @pl.when(g == 3)
        def _():
            part[i] = total[...]

        @pl.when(g == 2)
        def _():
            total[...] += part[i]

        @pl.when(g < 3)
        def _():
            send_sums(g, i, sign)

    def send_sums(g, i, sign):
        for d in range(2):

            @pl.when(i < 2)
            def _():
                rs_out[g, i, d] = total[d].astype(BF16)

            @pl.when((i >= 2) & (i < 7))
            def _():
                rs_copy(g, i - 2, d, ring(1)).wait_recv()
                rs_out[g, i, d] = (total[d] + rs_in[g, i - 2, d].astype(F32)).astype(BF16)

            @pl.when(i < 7)
            def _():
                rs_copy(g, i, d, ring(sign)).start()

        @pl.when(i == 7)
        def _():
            for d in range(2):
                for j in (5, 6):
                    rs_copy(g, j, d, ring(1)).wait_recv()
            total[...] = total[...] + rs_in[g, 5].astype(F32) + rs_in[g, 6].astype(F32)
            theirs = pl.ds(pl.multiple_of((1 - zh) * 128, 128), 128)
            mine = pl.ds(pl.multiple_of(zh * 128, 128), 128)
            rs_out[g, 7, :, 0:128] = total[:, theirs].astype(BF16)
            rs_z_copy(g).start()
            fin[g] = total[:, mine]

    def put(g, both):
        a, b, c = split3(both[0] * inv)
        full = dot(a, had[...]) + dot(b, had[...]) + dot(c, had[...])
        kg[g] = (full * inv).astype(BF16)
        vg[g] = both[1].astype(BF16)

    def finish(g):
        rs_z_copy(g).wait_recv()
        theirs = rs_in[g, 7, :, 0:128].astype(F32)
        if g < 2:
            put(g, fin[g] + theirs)
        else:
            put(split_g, fin[g])
            put(other_g, theirs)

    def slot(t, _):
        turn, i = t // NY, t % NY

        ag_own(t + AHEAD)

        def stat(g, at):
            stat_unit(g, at)
            return 0

        @pl.when(turn == 0)
        def _():
            lax.fori_loop(0, 2, lambda k, _: stat(k, i), 0)

        @pl.when((turn == 1) & (i == ROWS_AT))
        def _():
            take_rows()

        @pl.when(turn == 1)
        def _():
            late = i - ROWS_AT
            many = jnp.where((late >= 0) & (late < 2), 5, 1)
            lax.fori_loop(
                0, many,
                lambda k, _: stat(jnp.where(k == 0, 2, 3), jnp.where(k == 0, i, 4 * late + k - 1)),
                0,
            )

        ag_mate(t + AHEAD)

        @pl.when(turn > 0)
        def _():
            early = i - (ROWS_AT + 2)
            many = jnp.where(
                turn == 1, jnp.where(early >= 0, 3, 1), jnp.where(i < REST, 3, 2)
            )

            def one(k, _):
                g = jnp.where(turn == 1, jnp.where(k == 0, 0, 3), 1 + k)
                at = jnp.where(
                    turn == 1,
                    jnp.where(k == 0, i, 2 * early + k - 1),
                    jnp.where(k == 2, NY - REST + i, i),
                )
                grad_unit(g, at)
                return 0

            lax.fori_loop(0, many, one, 0)

        @pl.when(t == 2 * NY + 2)
        def _():
            finish(0)

        return 0

    lax.fori_loop(0, 3 * NY, slot, 0)

    @pl.when(pipe == n_pipe - 1)
    def _():
        for g in range(4):
            zero_copy(g).start()

    for g in range(1, 3):
        finish(g)

    @pl.when(pipe == n_pipe - 1)
    def _():
        for g in range(4):
            zero_copy(g).wait()

    @pl.when(pipe < n_pipe - 1)
    def _():
        for g in range(4):
            hand_copy(g).wait_recv()

    @pl.when(pipe > 0)
    def _():
        for g in range(4):
            hand_copy(g).wait_send()

    for copy in row_copies():
        copy.wait_send()
    for g in range(3):
        z_copy(g, ctx).wait_send()
        for half in range(2):
            for j in range(1, 8):
                ag_copy(g, half, j, ctx, ring(1)).wait_send()
        for j in range(7):
            for d in range(2):
                rs_copy(g, j, d, ring(1)).wait_send()
        rs_z_copy(g).wait_send()


def shards(queries, key_heads, value_heads, forward_out, output_grad, block_order):
    tok = queries.shape[1]
    k_in = key_heads[0].transpose(1, 0, 2)
    v_in = value_heads[0].transpose(1, 0, 2)
    had = jnp.asarray(signs(128), BF16)
    vmem = pl.BlockSpec(memory_space=pltpu.VMEM)
    hbm = pl.BlockSpec(memory_space=pl.ANY)
    dma = pltpu.SemaphoreType.DMA
    kg, vg, hand = pl.pallas_call(
        kernel,
        out_shape=(
            jax.ShapeDtypeStruct((4, tok, 128), BF16),
            jax.ShapeDtypeStruct((4, tok, 128), BF16),
            jax.ShapeDtypeStruct((4, 8 * tok, 128), BF16),
        ),
        in_specs=[pl.BlockSpec(memory_space=pltpu.SMEM), vmem, vmem, vmem, hbm, hbm, hbm],
        out_specs=(vmem, vmem, hbm),
        scratch_shapes=[
            pltpu.VMEM((tok, 32, 128), BF16),
            pltpu.VMEM((tok, 32, 128), BF16),
            pltpu.VMEM((tok, 32, 128), BF16),
            pltpu.VMEM((16, 4, 2, 128, 128), BF16),
            pltpu.VMEM((5, 1024, 128), BF16),
            pltpu.VMEM((5, 128, 1024), BF16),
            pltpu.VMEM((5, 1024, 128), BF16),
            pltpu.VMEM((5, 128, 1024), BF16),
            pltpu.VMEM((5, 8, 1024), F32),
            pltpu.VMEM((2, 8, 1024), jnp.int32),
            pltpu.VMEM((4, 8, 1024), F32),
            pltpu.VMEM((4, 8, 1024), F32),
            pltpu.VMEM((4, 8, 1024), F32),
            pltpu.VMEM((4, 16, 128, 1024), F32),
            pltpu.VMEM((256, 1024), BF16),
            pltpu.VMEM((256, 1024), BF16),
            pltpu.VMEM((4, 128, 1024), F32),
            pltpu.VMEM((3, 8, 2, 256, 128), BF16),
            pltpu.VMEM((3, 8, 2, 256, 128), BF16),
            pltpu.VMEM((8, 2, 256, 128), F32),
            pltpu.VMEM((2, 256, 128), F32),
            pltpu.VMEM((3, 2, 128, 128), F32),
            pltpu.VMEM((4, 1024, 128), BF16),
            pltpu.VMEM((1024, 128), BF16),
            dma((3,)),
            dma((3,)),
            dma((3,)),
            dma((3, 2, 8)),
            dma((3, 2, 8)),
            dma((3, 8, 2)),
            dma((3, 8, 2)),
            dma((4,)),
            dma((4,)),
        ],
        compiler_params=pltpu.CompilerParams(
            collective_id=0, has_side_effects=True, vmem_limit_bytes=60 * 1024 * 1024
        ),
        cost_estimate=pl.CostEstimate(
            flops=11_000_000_000, bytes_accessed=5_000_000, transcendentals=17_000_000
        ),
    )(block_order, k_in, v_in, had, queries[0], output_grad[0], forward_out[0])
    key_grad = kg.transpose(1, 0, 2)[None]
    value_grad = vg.transpose(1, 0, 2)[None]
    handed = hand.reshape(4, tok, 8, 128).transpose(1, 0, 2, 3).reshape(1, tok, 32, 128)
    return (key_grad, value_grad, handed)


def solution(mesh):
    placed = P("pipe", "ctx", "head", None)
    return jax.shard_map(
        shards,
        mesh=mesh,
        in_specs=(placed,) * 5 + (P(),),
        out_specs=(placed,) * 3,
        check_vma=False,
    )
```
